128 devices in a mesh: layer: 8 (over z, core), front: 16 (over y, x).
Axes of the slice: x: 4, y: 4, z: 4, core: 2. Of those that a mesh axis runs over, the one named last changes fastest.
Arguments:
- factor: bfloat16 [8, 2, 8192, 8192], P('layer', None, 'front'), may hold values from -0.046875 to 0.046875
- right_side: bfloat16 [8, 2, 8192, 256], P('layer', None, 'front'), may hold values from -6 to 6
- coupling: float32 [8, 8192], P('layer', 'front'), may hold values from 0.5 to 1.5
- forward: bfloat16 [8, 2, 8192, 256], P('layer', None, 'front'), may hold values from -6 to 6
Outputs:
- adjoint: bfloat16 [8, 2, 8192, 256], P('layer', None, 'front')
- gradient: float32 [8, 8192], P('layer', 'front')
The draws below stay inside these ranges and needn't reach their ends.
All inputs are finite; a program needn't handle non-finite values.
Results may differ from the reference program's by a relative error of at most 0.019.
Values may be sent and summed in bfloat16 or wider, within the bound.
No kernel may reach another device: no remote copies, remote signals or barrier semaphores. Data moves between devices by JAX's collectives and lax.ppermute only.
A program may use at most 128 MiB of HBM per device.

```python
import math
import jax
import jax.numpy as jnp
from jax import lax

FRONT = 8192
SOURCES = 256
LAYERS = 8


def level_of(rng, extent, cuts, low, high):
    def one(position, parts):
        heights = jax.random.uniform(jax.random.fold_in(jax.random.fold_in(rng, 6), position), (parts,), jnp.float32, low / len(cuts), high / len(cuts))
        return jnp.repeat(jnp.exp(heights), extent[position] // parts).reshape((-1,) + (1,) * (len(extent) - position - 1))

    loudness = one(*cuts[0])
    for cut in cuts[1:]:
        loudness = loudness * one(*cut)
    return loudness


def normal_values(rng, shape, deviation, most, pieces=(), dtype=jnp.bfloat16):
    array = deviation * jax.random.normal(rng, shape, jnp.float32)
    if pieces:
        array = array * level_of(rng, shape, pieces, -0.22, 0.18)
    return jnp.clip(array, -most, most).astype(dtype)


def setup_inputs(seed: int = 0) -> dict:
    seeds = jax.random.split(jax.random.key(seed), 5)
    return {
        "factor": normal_values(seeds[0], (LAYERS, 2, FRONT, FRONT), (2 * FRONT) ** -0.5, 0.046875, ((0, 8), (2, 16))),
        "right_side": normal_values(seeds[1], (LAYERS, 2, FRONT, SOURCES), 1.0, 6.0, ((0, 8), (2, 16))),
        "coupling": jnp.clip(0.5 + 1.0 * jax.random.uniform(seeds[2], (LAYERS, FRONT), jnp.float32) ** level_of(seeds[2], (LAYERS, FRONT), ((0, 8), (1, 16)), -0.2, 0.2), 0.5, 1.5),
        "forward": normal_values(seeds[3], (LAYERS, 2, FRONT, SOURCES), 1.0, 6.0, ((0, 8), (2, 16))),
    }


def reference(factor, right_side, coupling, forward):
    upper = jnp.zeros((2, FRONT, SOURCES), jnp.bfloat16)
    collected = []
    for layer_index in range(LAYERS - 1, -1, -1):
        merged = (right_side[layer_index].astype(jnp.float32) + coupling[layer_index][None, :, None] * upper.astype(jnp.float32)).astype(jnp.bfloat16)
        joined = jnp.concatenate((merged[0], merged[1]), axis=1)
        plain = jnp.dot(factor[layer_index, 0], joined, preferred_element_type=jnp.float32)
        twisted = jnp.dot(factor[layer_index, 1], joined, preferred_element_type=jnp.float32)
        real_part = plain[:, :SOURCES] - twisted[:, SOURCES:]
        imag_part = plain[:, SOURCES:] + twisted[:, :SOURCES]
        upper = jnp.stack((real_part, imag_part)).astype(jnp.bfloat16)
        collected.append(upper)
    adjoint = jnp.stack(collected[::-1])
    field_fwd = forward.astype(jnp.float32)
    field_adj = adjoint.astype(jnp.float32)
    gradient = lax.optimization_barrier(jnp.sum(field_fwd[:, 0] * field_adj[:, 0] - field_fwd[:, 1] * field_adj[:, 1], axis=-1)) / math.sqrt(SOURCES)
    return (adjoint, gradient)
```

```python
import math

import jax
import jax.numpy as jnp
from jax import lax
from jax.experimental import pallas as pl
from jax.experimental.pallas import tpu as pltpu
from jax.sharding import PartitionSpec as P

AXES = ("layer", "front")
BLOCKS = 4
SIDE = 4
IN_VMEM = pl.BlockSpec(memory_space=pltpu.VMEM)
IN_SMEM = pl.BlockSpec(memory_space=pltpu.SMEM)
IN_HBM = pl.BlockSpec(memory_space=pltpu.HBM)


def arrange(factor, order):
    rows, columns = factor.shape
    fronts = order.shape[0]
    width = columns // fronts

    def body(order_ref, source, target, sem):
        def copy(i):
            start = pl.multiple_of(order_ref[i] * width, width)
            return pltpu.make_async_copy(
                source.at[:, pl.ds(start, width)], target.at[:, pl.ds(i * width, width)], sem.at[i]
            )

        for i in range(fronts):
            copy(i).start()
        for i in range(fronts):
            copy(i).wait()

    return pl.pallas_call(
        body,
        in_specs=[IN_SMEM, IN_HBM],
        out_specs=IN_VMEM,
        out_shape=pltpu.VMEM((rows, columns), factor.dtype),
        scratch_shapes=[pltpu.SemaphoreType.DMA((fronts,))],
        compiler_params=pltpu.CompilerParams(vmem_limit_bytes=32 << 20),
        cost_estimate=pl.CostEstimate(flops=0, bytes_accessed=2 * rows * columns, transcendentals=0),
        name="arrange",
    )(order, factor)


def term(panel_ref, group, pieces):
    span = panel_ref.shape[1] // SIDE
    joined = jnp.concatenate([pieces[i] for i in range(SIDE)], axis=1)
    return lax.dot_general(
        panel_ref[:, group * span:(group + 1) * span],
        joined,
        (((1,), (1,)), ((), ())),
        preferred_element_type=jnp.float32,
    )


def start_product(panel, near):
    rows, columns = panel.shape
    height = near.shape[1]

    def body(panel_ref, near_ref, total_ref):
        total_ref[...] = term(panel_ref, 0, near_ref)

    return pl.pallas_call(
        body,
        in_specs=[IN_VMEM] * 2,
        out_specs=IN_VMEM,
        out_shape=jax.ShapeDtypeStruct((rows, height), jnp.float32),
        compiler_params=pltpu.CompilerParams(vmem_limit_bytes=16 << 20),
        cost_estimate=pl.CostEstimate(
            flops=rows * columns * height // 2, bytes_accessed=rows * columns // 2, transcendentals=0
        ),
        name="start_product",
    )(pltpu.with_memory_space_constraint(panel, pltpu.VMEM), near)


def finish_product(panel, total, groups, rhs, couple):
    rows, columns = panel.shape
    height = total.shape[1]
    half, middle = height // 2, rows // 2

    def body(panel_ref, total_ref, *refs):
        groups_refs = refs[:SIDE - 1]
        rhs_ref, couple_ref, field_ref, merged_ref, sum_ref = refs[SIDE - 1:]
        sum_ref[...] = total_ref[...]
        for i, group_ref in enumerate(groups_refs):
            sum_ref[...] += term(panel_ref, i + 1, group_ref)
        plain = sum_ref[:middle].T
        twisted = sum_ref[middle:].T
        field = jnp.concatenate(
            (plain[:half] - twisted[half:], plain[half:] + twisted[:half]), axis=0
        ).astype(field_ref.dtype)
        field_ref[...] = field
        merged = rhs_ref[...].astype(jnp.float32) + couple_ref[...] * field.astype(jnp.float32)
        merged_ref[...] = merged.astype(merged_ref.dtype)

    shape = jax.ShapeDtypeStruct((height, middle), jnp.bfloat16)
    return pl.pallas_call(
        body,
        in_specs=[IN_VMEM] * (SIDE + 3),
        out_specs=(IN_VMEM, IN_VMEM),
        out_shape=(shape, shape),
        scratch_shapes=[pltpu.VMEM((rows, height), jnp.float32)],
        compiler_params=pltpu.CompilerParams(vmem_limit_bytes=16 << 20),
        cost_estimate=pl.CostEstimate(
            flops=rows * columns * height * 3 // 2, bytes_accessed=rows * columns * 3 // 2, transcendentals=0
        ),
        name="finish_product",
    )(pltpu.with_memory_space_constraint(panel, pltpu.VMEM), total, *groups, rhs, couple)


def on_device(factor, right_side, coupling, forward):
    layers, fronts = lax.axis_size("layer"), lax.axis_size("front")
    position = lax.axis_index("layer")
    place = lax.axis_index("front")
    rows, sources = right_side.shape[2:]
    count = BLOCKS
    block = sources // count
    steps = count + layers - 1

    def device(layer, slow, fast):
        return layer % layers * fronts + slow % SIDE * SIDE + fast % SIDE

    def moves(down, near, far):
        pairs = []
        for layer in range(layers):
            reached = (layer - down) % layers
            slow_step, fast_step = (far, near) if reached % 2 == 0 else (near, far)
            for slow in range(SIDE):
                for fast in range(SIDE):
                    pairs.append(
                        (device(layer, slow, fast), device(reached, slow + slow_step, fast + fast_step))
                    )
        return pairs

    def moved(value, down, near, far):
        return lax.ppermute(value, AXES, moves(down, near, far))

    slow, fast = place // SIDE, place % SIDE
    even = position % 2 == 0
    order = []
    for far in range(SIDE):
        for near in range(SIDE):
            slow_step = jnp.where(even, far, near)
            fast_step = jnp.where(even, near, far)
            order.append((slow - slow_step) % SIDE * SIDE + (fast - fast_step) % SIDE)
    order = jnp.stack(order).astype(jnp.int32)
    panel = arrange(factor[0].reshape(2 * rows, -1), order)

    turned = jnp.swapaxes(right_side[0], 1, 2)
    blocks = turned.reshape(2, count, block, rows).swapaxes(0, 1).reshape(count, 2 * block, rows)

    up = [(l * fronts + f, (l + 1) % layers * fronts + f) for l in range(layers) for f in range(fronts)]
    next_rhs = lax.ppermute(blocks, AXES, up)
    next_couple = jnp.where(position == 0, 0.0, lax.ppermute(coupling, AXES, up))
    depth = jnp.where(position == 0, layers, position)
    next_rhs = jnp.pad(next_rhs, ((layers - 2, layers - 1), (0, 0), (0, 0)))
    next_rhs = lax.dynamic_slice_in_dim(next_rhs, depth - 1, steps - 1, 0)

    fields = []
    merged = blocks[0]
    for step in range(steps):
        down = min(step, 1)
        near = jnp.stack([merged if down == 0 and i == 0 else moved(merged, down, i, 0) for i in range(SIDE)])
        far = [moved(near, 0, 0, i) for i in range(1, SIDE)]
        total = start_product(panel, near)
        rhs = next_rhs[min(step, steps - 2)]
        field, merged = finish_product(panel, total, far, rhs, next_couple)
        fields.append(field)

    result = lax.dynamic_slice_in_dim(jnp.stack(fields), layers - 1 - position, count, 0)
    result = result.reshape(count, 2, block, rows).swapaxes(0, 1).reshape(2, sources, rows)
    result = jnp.swapaxes(result, 1, 2)
    field_fwd = forward[0].astype(jnp.float32)
    field_adj = result.astype(jnp.float32)
    gradient = jnp.sum(
        field_fwd[0] * field_adj[0] - field_fwd[1] * field_adj[1], axis=-1
    ) / math.sqrt(sources)
    return (result[None], gradient[None])


def solution(mesh):
    placed = (
        P("layer", None, "front", None),
        P("layer", None, "front", None),
        P("layer", "front"),
        P("layer", None, "front", None),
    )
    return jax.shard_map(
        on_device,
        mesh=mesh,
        in_specs=placed,
        out_specs=(P("layer", None, "front", None), P("layer", "front")),
        check_vma=False,
    )
```

```python
import math

import jax
import jax.numpy as jnp
from jax import lax
from jax.experimental import pallas as pl
from jax.experimental.pallas import tpu as pltpu
from jax.sharding import PartitionSpec as P

AXES = ("layer", "front")
BLOCKS = 4
HOP_FIRST = False
NEAR_ORDER = (1, 3, 2, 0)
FAR_ORDER = (2, 3, 1)
USE_ORDER = (1, 3, 2)
SIDE = 4
IN_VMEM = pl.BlockSpec(memory_space=pltpu.VMEM)
IN_SMEM = pl.BlockSpec(memory_space=pltpu.SMEM)
IN_HBM = pl.BlockSpec(memory_space=pltpu.HBM)


def arrange(factor, order):
    rows, columns = factor.shape
    fronts = order.shape[0]
    width = columns // fronts

    def body(order_ref, source, *refs):
        targets, sem = refs[:SIDE], refs[SIDE]

        def copy(i):
            start = pl.multiple_of(order_ref[i] * width, width)
            return pltpu.make_async_copy(
                source.at[:, pl.ds(start, width)],
                targets[i // SIDE].at[:, pl.ds(i % SIDE * width, width)],
                sem.at[i],
            )

        for i in range(fronts):
            copy(i).start()
        for i in range(fronts):
            copy(i).wait()

    return pl.pallas_call(
        body,
        in_specs=[IN_SMEM, IN_HBM],
        out_specs=(IN_VMEM,) * SIDE,
        out_shape=(pltpu.VMEM((rows, columns // SIDE), factor.dtype),) * SIDE,
        scratch_shapes=[pltpu.SemaphoreType.DMA((fronts,))],
        compiler_params=pltpu.CompilerParams(vmem_limit_bytes=32 << 20),
        cost_estimate=pl.CostEstimate(flops=0, bytes_accessed=2 * rows * columns, transcendentals=0),
        name="arrange",
    )(order, factor)


def kept(value):
    return pltpu.with_memory_space_constraint(value, pltpu.VMEM)


def term(panel_ref, pieces_ref):
    joined = jnp.concatenate([pieces_ref[i] for i in range(SIDE)], axis=1)
    return lax.dot_general(
        panel_ref[...], joined, (((1,), (1,)), ((), ())), preferred_element_type=jnp.float32
    )


def add_product(panel, total, pieces):
    rows, columns = panel.shape
    height = pieces.shape[1]
    totals = () if total is None else (kept(total),)

    def body(panel_ref, pieces_ref, *refs):
        product = term(panel_ref, pieces_ref)
        refs[-1][...] = product if total is None else refs[0][...] + product

    return pl.pallas_call(
        body,
        in_specs=[IN_VMEM] * (2 + len(totals)),
        out_specs=IN_VMEM,
        out_shape=pltpu.VMEM((rows, height), jnp.float32),
        compiler_params=pltpu.CompilerParams(vmem_limit_bytes=16 << 20),
        cost_estimate=pl.CostEstimate(
            flops=2 * rows * columns * height, bytes_accessed=2 * rows * columns, transcendentals=0
        ),
        name="add_product",
    )(kept(panel), pieces, *totals)


def finish_product(panel, total, pieces, rhs, couple):
    rows, columns = panel.shape
    height = total.shape[1]
    half, middle = height // 2, rows // 2

    def body(panel_ref, total_ref, pieces_ref, rhs_ref, couple_ref, field_ref, merged_ref):
        total = total_ref[...] + term(panel_ref, pieces_ref)
        plain = total[:middle].T
        twisted = total[middle:].T
        field = jnp.concatenate(
            (plain[:half] - twisted[half:], plain[half:] + twisted[:half]), axis=0
        ).astype(field_ref.dtype)
        field_ref[...] = field
        merged = rhs_ref[...].astype(jnp.float32) + couple_ref[...] * field.astype(jnp.float32)
        merged_ref[...] = merged.astype(merged_ref.dtype)

    shape = jax.ShapeDtypeStruct((height, middle), jnp.bfloat16)
    return pl.pallas_call(
        body,
        in_specs=[IN_VMEM] * 5,
        out_specs=(IN_VMEM, IN_VMEM),
        out_shape=(shape, shape),
        compiler_params=pltpu.CompilerParams(vmem_limit_bytes=16 << 20),
        cost_estimate=pl.CostEstimate(
            flops=2 * rows * columns * height, bytes_accessed=2 * rows * columns, transcendentals=0
        ),
        name="finish_product",
    )(kept(panel), kept(total), pieces, rhs, couple)


def on_device(factor, right_side, coupling, forward):
    layers, fronts = lax.axis_size("layer"), lax.axis_size("front")
    position = lax.axis_index("layer")
    place = lax.axis_index("front")
    rows, sources = right_side.shape[2:]
    count = BLOCKS
    block = sources // count
    steps = count + layers - 1

    def device(layer, slow, fast):
        return layer * fronts + slow * SIDE + fast

    def moves(down, near, far):
        pairs = []
        for layer in range(layers):
            reached = (layer - down) % layers
            slow_step, fast_step = (far, near) if reached % 2 == 0 else (near, far)
            for slow in range(SIDE):
                for fast in range(SIDE):
                    pairs.append(
                        (device(layer, slow, fast), device(reached, slow ^ slow_step, fast ^ fast_step))
                    )
        return pairs

    def moved(value, down, near, far):
        return lax.ppermute(value, AXES, moves(down, near, far))

    slow, fast = place // SIDE, place % SIDE
    even = position % 2 == 0
    order = []
    for far in range(SIDE):
        for near in range(SIDE):
            slow_step = jnp.where(even, far, near)
            fast_step = jnp.where(even, near, far)
            order.append((slow ^ slow_step) * SIDE + (fast ^ fast_step))
    order = jnp.stack(order).astype(jnp.int32)
    panels = arrange(factor[0].reshape(2 * rows, -1), order)

    turned = jnp.swapaxes(right_side[0], 1, 2)
    blocks = turned.reshape(2, count, block, rows).swapaxes(0, 1).reshape(count, 2 * block, rows)

    up = [(l * fronts + f, (l + 1) % layers * fronts + f) for l in range(layers) for f in range(fronts)]
    next_rhs = lax.ppermute(blocks, AXES, up)
    next_couple = jnp.where(position == 0, 0.0, lax.ppermute(coupling, AXES, up))
    depth = jnp.where(position == 0, layers, position)
    next_rhs = jnp.pad(next_rhs, ((layers - 2, layers - 1), (0, 0), (0, 0)))
    next_rhs = lax.dynamic_slice_in_dim(next_rhs, depth - 1, steps - 1, 0)

    fields = []
    merged = blocks[0]
    for step in range(steps):
        down = min(step, 1)
        if HOP_FIRST:
            own = moved(merged, 1, 0, 0) if down else merged
            near = {0: own} | {i: moved(own, 0, i, 0) for i in NEAR_ORDER if i}
        else:
            near = {i: merged if down == 0 and i == 0 else moved(merged, down, i, 0) for i in NEAR_ORDER}
        near = jnp.stack([near[i] for i in range(SIDE)])
        far = {i: moved(near, 0, 0, i) for i in FAR_ORDER}
        total = add_product(panels[0], None, near)
        for i in USE_ORDER[:-1]:
            total = add_product(panels[i], total, far[i])
        last = USE_ORDER[-1]
        rhs = next_rhs[min(step, steps - 2)]
        field, merged = finish_product(panels[last], total, far[last], rhs, next_couple)
        fields.append(field)

    result = lax.dynamic_slice_in_dim(jnp.stack(fields), layers - 1 - position, count, 0)
    result = result.reshape(count, 2, block, rows).swapaxes(0, 1).reshape(2, sources, rows)
    result = jnp.swapaxes(result, 1, 2)
    forward, result = lax.optimization_barrier((forward, result))
    field_fwd = forward[0].astype(jnp.float32)
    field_adj = result.astype(jnp.float32)
    gradient = jnp.sum(
        field_fwd[0] * field_adj[0] - field_fwd[1] * field_adj[1], axis=-1
    ) / math.sqrt(sources)
    return (result[None], gradient[None])


def solution(mesh):
    placed = (
        P("layer", None, "front", None),
        P("layer", None, "front", None),
        P("layer", "front"),
        P("layer", None, "front", None),
    )
    return jax.shard_map(
        on_device,
        mesh=mesh,
        in_specs=placed,
        out_specs=(P("layer", None, "front", None), P("layer", "front")),
        check_vma=False,
    )
```

```python
import math

import jax
import jax.numpy as jnp
from jax import lax
from jax.experimental import pallas as pl
from jax.experimental.pallas import tpu as pltpu
from jax.sharding import PartitionSpec as P

AXES = ("layer", "front")
BLOCKS = 4
NEAR_ORDER = (1, 3, 2, 0)
SIDE = 4
IN_VMEM = pl.BlockSpec(memory_space=pltpu.VMEM)
IN_SMEM = pl.BlockSpec(memory_space=pltpu.SMEM)
IN_HBM = pl.BlockSpec(memory_space=pltpu.HBM)


def arrange(factor, order):
    rows, columns = factor.shape
    fronts = order.shape[0]
    width = columns // fronts

    def body(order_ref, source, *refs):
        targets, sem = refs[:SIDE], refs[SIDE]

        def copy(i):
            start = pl.multiple_of(order_ref[i] * width, width)
            return pltpu.make_async_copy(
                source.at[:, pl.ds(start, width)],
                targets[i // SIDE].at[:, pl.ds(i % SIDE * width, width)],
                sem.at[i],
            )

        for i in range(fronts):
            copy(i).start()
        for i in range(fronts):
            copy(i).wait()

    return pl.pallas_call(
        body,
        in_specs=[IN_SMEM, IN_HBM],
        out_specs=(IN_VMEM,) * SIDE,
        out_shape=(pltpu.VMEM((rows, columns // SIDE), factor.dtype),) * SIDE,
        scratch_shapes=[pltpu.SemaphoreType.DMA((fronts,))],
        compiler_params=pltpu.CompilerParams(vmem_limit_bytes=32 << 20),
        cost_estimate=pl.CostEstimate(flops=0, bytes_accessed=2 * rows * columns, transcendentals=0),
        name="arrange",
    )(order, factor)


def kept(value):
    return pltpu.with_memory_space_constraint(value, pltpu.VMEM)


def term(panel_ref, *pieces_refs):
    joined = jnp.concatenate([ref[i] for ref in pieces_refs for i in range(ref.shape[0])], axis=1)
    return lax.dot_general(
        panel_ref[...], joined, (((1,), (1,)), ((), ())), preferred_element_type=jnp.float32
    )


def add_product(panel, total, first, second):
    rows, columns = panel.shape
    height = first.shape[1]
    totals = () if total is None else (kept(total),)

    def body(panel_ref, first_ref, second_ref, *refs):
        product = term(panel_ref, first_ref, second_ref)
        refs[-1][...] = product if total is None else refs[0][...] + product

    return pl.pallas_call(
        body,
        in_specs=[IN_VMEM] * (3 + len(totals)),
        out_specs=IN_VMEM,
        out_shape=pltpu.VMEM((rows, height), jnp.float32),
        compiler_params=pltpu.CompilerParams(vmem_limit_bytes=16 << 20),
        cost_estimate=pl.CostEstimate(
            flops=2 * rows * columns * height, bytes_accessed=2 * rows * columns, transcendentals=0
        ),
        name="add_product",
    )(kept(panel), first, second, *totals)


def finish_product(panel, total, first, second, rhs, couple):
    rows, columns = panel.shape
    height = total.shape[1]
    half, middle = height // 2, rows // 2

    def body(panel_ref, total_ref, first_ref, second_ref, rhs_ref, couple_ref, field_ref, merged_ref):
        total = total_ref[...] + term(panel_ref, first_ref, second_ref)
        plain = total[:middle].T
        twisted = total[middle:].T
        field = jnp.concatenate(
            (plain[:half] - twisted[half:], plain[half:] + twisted[:half]), axis=0
        ).astype(field_ref.dtype)
        field_ref[...] = field
        merged = rhs_ref[...].astype(jnp.float32) + couple_ref[...] * field.astype(jnp.float32)
        merged_ref[...] = merged.astype(merged_ref.dtype)

    shape = jax.ShapeDtypeStruct((height, middle), jnp.bfloat16)
    return pl.pallas_call(
        body,
        in_specs=[IN_VMEM] * 6,
        out_specs=(IN_VMEM, IN_VMEM),
        out_shape=(shape, shape),
        compiler_params=pltpu.CompilerParams(vmem_limit_bytes=16 << 20),
        cost_estimate=pl.CostEstimate(
            flops=2 * rows * columns * height, bytes_accessed=2 * rows * columns, transcendentals=0
        ),
        name="finish_product",
    )(kept(panel), kept(total), first, second, rhs, couple)


def on_device(factor, right_side, coupling, forward):
    layers, fronts = lax.axis_size("layer"), lax.axis_size("front")
    position = lax.axis_index("layer")
    place = lax.axis_index("front")
    rows, sources = right_side.shape[2:]
    count = BLOCKS
    block = sources // count
    steps = count + layers - 1

    def device(layer, slow, fast):
        return layer * fronts + slow * SIDE + fast

    def moves(down, near, far):
        pairs = []
        for layer in range(layers):
            reached = (layer - down) % layers
            slow_step, fast_step = (far, near) if reached % 2 == 0 else (near, far)
            for slow in range(SIDE):
                for fast in range(SIDE):
                    pairs.append(
                        (device(layer, slow, fast), device(reached, slow ^ slow_step, fast ^ fast_step))
                    )
        return pairs

    def moved(value, down, near, far):
        return lax.ppermute(value, AXES, moves(down, near, far))

    slow, fast = place // SIDE, place % SIDE
    even = position % 2 == 0
    order = []
    for far in range(SIDE):
        for near in range(SIDE):
            slow_step = jnp.where(even, far, near)
            fast_step = jnp.where(even, near, far)
            order.append((slow ^ slow_step) * SIDE + (fast ^ fast_step))
    order = jnp.stack(order).astype(jnp.int32)
    panels = arrange(factor[0].reshape(2 * rows, -1), order)

    turned = jnp.swapaxes(right_side[0], 1, 2)
    blocks = turned.reshape(2, count, block, rows).swapaxes(0, 1).reshape(count, 2 * block, rows)

    up = [(l * fronts + f, (l + 1) % layers * fronts + f) for l in range(layers) for f in range(fronts)]
    next_rhs = lax.ppermute(blocks, AXES, up)
    next_couple = jnp.where(position == 0, 0.0, lax.ppermute(coupling, AXES, up))
    depth = jnp.where(position == 0, layers, position)
    next_rhs = jnp.pad(next_rhs, ((layers - 2, layers - 1), (0, 0), (0, 0)))
    next_rhs = lax.dynamic_slice_in_dim(next_rhs, depth - 1, steps - 1, 0)

    fields = []
    merged = blocks[0]
    for step in range(steps):
        down = min(step, 1)
        near = {i: merged if down == 0 and i == 0 else moved(merged, down, i, 0) for i in NEAR_ORDER}
        low = jnp.stack([near[0], near[1]])
        high = jnp.stack([near[2], near[3]])
        behind_low, ahead_high = moved(low, 0, 0, 1), moved(high, 0, 0, 3)
        behind_high, ahead_low = moved(high, 0, 0, 1), moved(low, 0, 0, 3)
        across_low, across_high = moved(behind_low, 0, 0, 3), moved(ahead_high, 0, 0, 1)
        total = add_product(panels[0], None, low, high)
        total = add_product(panels[1], total, behind_low, behind_high)
        total = add_product(panels[3], total, ahead_low, ahead_high)
        rhs = next_rhs[min(step, steps - 2)]
        field, merged = finish_product(panels[2], total, across_low, across_high, rhs, next_couple)
        fields.append(field)

    fields = lax.optimization_barrier(fields)
    result = lax.dynamic_slice_in_dim(jnp.stack(fields), layers - 1 - position, count, 0)
    result = result.reshape(count, 2, block, rows).swapaxes(0, 1).reshape(2, sources, rows)
    result = jnp.swapaxes(result, 1, 2)
    forward, result = lax.optimization_barrier((forward, result))
    field_fwd = forward[0].astype(jnp.float32)
    field_adj = result.astype(jnp.float32)
    gradient = jnp.sum(
        field_fwd[0] * field_adj[0] - field_fwd[1] * field_adj[1], axis=-1
    ) / math.sqrt(sources)
    return (result[None], gradient[None])


def solution(mesh):
    placed = (
        P("layer", None, "front", None),
        P("layer", None, "front", None),
        P("layer", "front"),
        P("layer", None, "front", None),
    )
    return jax.shard_map(
        on_device,
        mesh=mesh,
        in_specs=placed,
        out_specs=(P("layer", None, "front", None), P("layer", "front")),
        check_vma=False,
    )
```

```python
import math

import jax
import jax.numpy as jnp
from jax import lax
from jax.experimental import pallas as pl
from jax.experimental.pallas import tpu as pltpu
from jax.sharding import PartitionSpec as P

AXES = ("layer", "front")
BLOCKS = 4
NEAR_ORDER = (1, 3, 2, 0)
SIDE = 4
IN_VMEM = pl.BlockSpec(memory_space=pltpu.VMEM)
IN_SMEM = pl.BlockSpec(memory_space=pltpu.SMEM)
IN_HBM = pl.BlockSpec(memory_space=pltpu.HBM)


def arrange(factor, order):
    rows, columns = factor.shape
    fronts = order.shape[0]
    width = columns // fronts

    def body(order_ref, source, *refs):
        targets, sem = refs[:SIDE], refs[SIDE]

        def copy(i):
            start = pl.multiple_of(order_ref[i] * width, width)
            return pltpu.make_async_copy(
                source.at[:, pl.ds(start, width)],
                targets[i // SIDE].at[:, pl.ds(i % SIDE * width, width)],
                sem.at[i],
            )

        for i in range(fronts):
            copy(i).start()
        for i in range(fronts):
            copy(i).wait()

    return pl.pallas_call(
        body,
        in_specs=[IN_SMEM, IN_HBM],
        out_specs=(IN_VMEM,) * SIDE,
        out_shape=(pltpu.VMEM((rows, columns // SIDE), factor.dtype),) * SIDE,
        scratch_shapes=[pltpu.SemaphoreType.DMA((fronts,))],
        compiler_params=pltpu.CompilerParams(vmem_limit_bytes=32 << 20),
        cost_estimate=pl.CostEstimate(flops=0, bytes_accessed=2 * rows * columns, transcendentals=0),
        name="arrange",
    )(order, factor)


def kept(value):
    return pltpu.with_memory_space_constraint(value, pltpu.VMEM)


def term(panel_ref, *pieces_refs):
    joined = jnp.concatenate([ref[i] for ref in pieces_refs for i in range(ref.shape[0])], axis=1)
    return lax.dot_general(
        panel_ref[...], joined, (((1,), (1,)), ((), ())), preferred_element_type=jnp.float32
    )


def add_product(panel, total, first, second):
    rows, columns = panel.shape
    height = first.shape[1]
    totals = () if total is None else (kept(total),)

    def body(panel_ref, first_ref, second_ref, *refs):
        product = term(panel_ref, first_ref, second_ref)
        refs[-1][...] = product if total is None else refs[0][...] + product

    return pl.pallas_call(
        body,
        in_specs=[IN_VMEM] * (3 + len(totals)),
        out_specs=IN_VMEM,
        out_shape=pltpu.VMEM((rows, height), jnp.float32),
        compiler_params=pltpu.CompilerParams(vmem_limit_bytes=16 << 20),
        cost_estimate=pl.CostEstimate(
            flops=2 * rows * columns * height, bytes_accessed=2 * rows * columns, transcendentals=0
        ),
        name="add_product",
    )(kept(panel), first, second, *totals)


def finish_product(panel, total, first, second, rhs, couple):
    rows, columns = panel.shape
    height = total.shape[1]
    half, middle = height // 2, rows // 2

    def body(panel_ref, total_ref, first_ref, second_ref, rhs_ref, couple_ref, field_ref, merged_ref):
        total = total_ref[...] + term(panel_ref, first_ref, second_ref)
        plain = total[:middle].T
        twisted = total[middle:].T
        field = jnp.concatenate(
            (plain[:half] - twisted[half:], plain[half:] + twisted[:half]), axis=0
        ).astype(field_ref.dtype)
        field_ref[...] = field
        merged = rhs_ref[...].astype(jnp.float32) + couple_ref[...] * field.astype(jnp.float32)
        merged_ref[...] = merged.astype(merged_ref.dtype)

    shape = jax.ShapeDtypeStruct((height, middle), jnp.bfloat16)
    return pl.pallas_call(
        body,
        in_specs=[IN_VMEM] * 6,
        out_specs=(IN_VMEM, IN_VMEM),
        out_shape=(shape, shape),
        compiler_params=pltpu.CompilerParams(vmem_limit_bytes=16 << 20),
        cost_estimate=pl.CostEstimate(
            flops=2 * rows * columns * height, bytes_accessed=2 * rows * columns, transcendentals=0
        ),
        name="finish_product",
    )(kept(panel), kept(total), first, second, rhs, couple)


def rows_from(array, start, count):
    zero = jnp.zeros((), start.dtype)
    return lax.dynamic_slice(
        array, (start, zero, zero), (count, *array.shape[1:]), allow_negative_indices=False
    )


def on_device(factor, right_side, coupling, forward):
    layers, fronts = lax.axis_size("layer"), lax.axis_size("front")
    position = lax.axis_index("layer")
    place = lax.axis_index("front")
    rows, sources = right_side.shape[2:]
    count = BLOCKS
    block = sources // count
    steps = count + layers - 1

    def device(layer, slow, fast):
        return layer * fronts + slow * SIDE + fast

    def moves(down, near, far):
        pairs = []
        for layer in range(layers):
            reached = (layer - down) % layers
            slow_step, fast_step = (far, near) if reached % 2 == 0 else (near, far)
            for slow in range(SIDE):
                for fast in range(SIDE):
                    pairs.append(
                        (device(layer, slow, fast), device(reached, slow ^ slow_step, fast ^ fast_step))
                    )
        return pairs

    def moved(value, down, near, far):
        return lax.ppermute(value, AXES, moves(down, near, far))

    slow, fast = place // SIDE, place % SIDE
    even = position % 2 == 0
    order = []
    for far in range(SIDE):
        for near in range(SIDE):
            slow_step = jnp.where(even, far, near)
            fast_step = jnp.where(even, near, far)
            order.append((slow ^ slow_step) * SIDE + (fast ^ fast_step))
    depth = jnp.where(position == 0, layers, position)
    order, first_rhs, first_live, is_top = lax.optimization_barrier(
        (jnp.stack(order).astype(jnp.int32), depth - 1, layers - 1 - position, position == 0)
    )
    panels = arrange(factor[0].reshape(2 * rows, -1), order)

    turned = jnp.swapaxes(right_side[0], 1, 2)
    blocks = turned.reshape(2, count, block, rows).swapaxes(0, 1).reshape(count, 2 * block, rows)

    up = [(l * fronts + f, (l + 1) % layers * fronts + f) for l in range(layers) for f in range(fronts)]
    next_rhs = lax.ppermute(blocks, AXES, up)
    next_couple = jnp.where(is_top, 0.0, lax.ppermute(coupling, AXES, up))
    next_rhs = jnp.pad(next_rhs, ((layers - 2, layers - 1), (0, 0), (0, 0)))
    next_rhs = lax.optimization_barrier(rows_from(next_rhs, first_rhs, steps - 1))

    fields = []
    merged = blocks[0]
    for step in range(steps):
        down = min(step, 1)
        near = {i: merged if down == 0 and i == 0 else moved(merged, down, i, 0) for i in NEAR_ORDER}
        low = jnp.stack([near[0], near[1]])
        high = jnp.stack([near[2], near[3]])
        behind_low, ahead_high = moved(low, 0, 0, 1), moved(high, 0, 0, 3)
        behind_high, ahead_low = moved(high, 0, 0, 1), moved(low, 0, 0, 3)
        across_low, across_high = moved(behind_low, 0, 0, 3), moved(ahead_high, 0, 0, 1)
        total = add_product(panels[0], None, low, high)
        total = add_product(panels[1], total, behind_low, behind_high)
        total = add_product(panels[3], total, ahead_low, ahead_high)
        rhs = next_rhs[min(step, steps - 2)]
        field, merged = finish_product(panels[2], total, across_low, across_high, rhs, next_couple)
        fields.append(field)

    fields = lax.optimization_barrier(fields)
    result = rows_from(jnp.stack(fields), first_live, count)
    result = result.reshape(count, 2, block, rows).swapaxes(0, 1).reshape(2, sources, rows)
    result = jnp.swapaxes(result, 1, 2)
    forward, result = lax.optimization_barrier((forward, result))
    field_fwd = forward[0].astype(jnp.float32)
    field_adj = result.astype(jnp.float32)
    gradient = jnp.sum(
        field_fwd[0] * field_adj[0] - field_fwd[1] * field_adj[1], axis=-1
    ) / math.sqrt(sources)
    return (result[None], gradient[None])


def solution(mesh):
    placed = (
        P("layer", None, "front", None),
        P("layer", None, "front", None),
        P("layer", "front"),
        P("layer", None, "front", None),
    )
    return jax.shard_map(
        on_device,
        mesh=mesh,
        in_specs=placed,
        out_specs=(P("layer", None, "front", None), P("layer", "front")),
        check_vma=False,
    )
```
